32 devices in a mesh: grp: 2 (over y), row: 16 (over z, x, core).
Axes of the slice: x: 2, y: 2, z: 4, core: 2. Of those that a mesh axis runs over, the one named last changes fastest.
Arguments:
- sensing: float32 [3072, 16384], P('row')
- measured: float32 [1536], P(('grp', 'row')), parts along dimension 0, may hold values from -6 to 6
- thresholds: float32 [12], P('grp'), parts along dimension 0, may hold values from 3 to 4
Outputs:
- estimate: float32 [131072], P(('grp', 'row')), parts along dimension 0
- residual: float32 [1536], P(('grp', 'row')), parts along dimension 0
The draws below stay inside these ranges and needn't reach their ends.
There are 2 independent parts, one for each index of `grp`. The reference program is written for one: setup_inputs(seed, part) draws one part's arguments, and reference() takes and returns one part's arrays. A program takes and returns all parts, laid end to end along the dimension named above; an argument that names none is the same for every part. Nothing has to cross between parts.
All inputs are finite; a program needn't handle non-finite values.
Results may differ from the reference program's by a relative error of at most 0.0003.
Values sent between devices are 32-bit elements; how exact they have to be, the bound alone decides.
No kernel may reach another device: no remote copies, remote signals or barrier semaphores. Data moves between devices by JAX's collectives and lax.ppermute only.
A program may use at most 64 MiB of HBM per device.

```python
import math
import jax
import jax.numpy as jnp
from jax import lax

N = 65536
COLS = 4
ROWS_DEV = 48
ITERS = 6
M = 768
N_ROW = 16


def draw_sensing(key, part):
    positions = jnp.arange(N, dtype=jnp.float32) / N
    entries = jax.random.normal(jax.random.fold_in(key, 13), (M, N), jnp.float32)
    jitter = jax.random.uniform(jax.random.fold_in(key, 14), (N,), jnp.float32, 0.8, 1.25)
    column_scale = 0.5 * jnp.exp(positions * math.log(3.0)) * jitter
    matrix = entries * column_scale[None, :] / math.sqrt(M)
    groups = M // ROWS_DEV // COLS
    width = N // COLS
    blocks = matrix.reshape(COLS, groups, ROWS_DEV, COLS, width).transpose(3, 1, 0, 2, 4)
    return blocks.reshape(M * COLS, width)


def levels(stream_key, dims, split, low, high):
    gain = 1.0
    for axis_at, shards_of in split:
        draws = jax.random.uniform(jax.random.fold_in(jax.random.fold_in(stream_key, 6), axis_at), (shards_of,), jnp.float32, low / len(split), high / len(split))
        gain = gain * jnp.repeat(jnp.exp(draws), dims[axis_at] // shards_of).reshape((-1,) + (1,) * (len(dims) - 1 - axis_at))
    return gain


def bell_draw(stream_key, shape, scale, limit, split=(), kind=jnp.bfloat16):
    values = scale * jax.random.normal(stream_key, shape, jnp.float32)
    if split:
        values = values * levels(stream_key, shape, split, -0.22, 0.18)
    return jnp.clip(values, -limit, limit).astype(kind)


def setup_inputs(seed: int = 0, part: int = 0) -> dict:
    streams_of = jax.random.split(jax.random.key(seed), 4)
    part_splits = jax.random.split(jax.random.fold_in(streams_of[3], part), 4)
    sensing = draw_sensing(jax.random.fold_in(streams_of[3], 71), part)
    measured = bell_draw(part_splits[1], (M,), 1.0, 6.0, ((0, 16),), jnp.float32)
    thresholds = jnp.clip(jax.random.uniform(part_splits[2], (ITERS,), jnp.float32, 3.0, 4.0), 3.0, 4.0)
    return dict(sensing=sensing, measured=measured, thresholds=thresholds)


SOFTNESS = 0.25


def shrink(values, level):
    return SOFTNESS * (jax.nn.softplus((values - level) / SOFTNESS) - jax.nn.softplus((-values - level) / SOFTNESS))


def slopes(values, level):
    return jax.nn.sigmoid((values - level) / SOFTNESS) + jax.nn.sigmoid((-values - level) / SOFTNESS)


def reference(sensing, measured, thresholds):
    groups = N_ROW // COLS
    width = N // COLS
    matrix = sensing.reshape(COLS, groups, COLS, ROWS_DEV, width).transpose(2, 1, 3, 0, 4).reshape(M, N)
    estimate = jnp.zeros((N,), jnp.float32)
    residual = measured
    for step in range(ITERS):
        pseudo = estimate + jnp.dot(residual, matrix, precision=lax.Precision.HIGHEST, preferred_element_type=jnp.float32)
        onsager = jnp.sum(slopes(pseudo, thresholds[step])) / M
        estimate = shrink(pseudo, thresholds[step])
        product = jnp.dot(matrix, estimate, precision=lax.Precision.HIGHEST, preferred_element_type=jnp.float32)
        residual = measured - product + onsager * residual
    return estimate, residual
```

```python
import functools

import jax
import jax.numpy as jnp
from jax import lax
from jax.experimental import pallas as pl
from jax.experimental.pallas import tpu as pltpu
from jax.sharding import PartitionSpec as P

COLS = 4
ITERS = 6
SOFTNESS = 0.25
LANES = 128
UNROLL = 16
VMEM = pltpu.VMEM
LIMIT = 40 * 2**20
ATANH = (
    0.999999999783453,
    0.3333334145023831,
    0.1999927837517024,
    0.14311218617609153,
    0.10693692054721207,
    0.1220053340626646,
)


def swapped(value, mask):
    pairs = [(source, source ^ mask) for source in range(lax.axis_size("row"))]
    return lax.ppermute(value, "row", pairs)


def shrink_and_slope(values, level):
    scaled = jnp.abs(values) * (1.0 / SOFTNESS)
    scaled_level = level * (1.0 / SOFTNESS)
    gap = scaled - scaled_level
    upper = jnp.exp(-jnp.abs(gap))
    lower = jnp.exp(-(scaled + scaled_level))
    one, two = 1.0 + upper, 2.0 + upper
    inverse = 1.0 / (one * two)
    ratio = upper * (one * inverse)
    square = ratio * ratio
    series = ATANH[-1]
    for coefficient in ATANH[-2::-1]:
        series = series * square + coefficient
    upper_log = (ratio + ratio) * series
    lower_log = lower * (1.0 - lower * (0.5 - lower * (1.0 / 3.0)))
    size = SOFTNESS * (jnp.maximum(gap, 0.0) + (upper_log - lower_log))
    estimate = jnp.where(values < 0.0, -size, jnp.where(values > 0.0, size, 0.0))
    slope = jnp.where(gap >= 0.0, 1.0, upper) * (two * inverse) + lower * (1.0 - lower * (1.0 - lower))
    return estimate, slope


def load_kernel(source, target, semaphore):
    copy = pltpu.make_async_copy(source, target, semaphore)
    copy.start()
    copy.wait()


def back_kernel(first, rows, all_rows, *refs):
    if first:
        *parts, sensing, out, residual_out = refs
    else:
        *parts, measured, old, sensing, out, residual_out = refs
    total = parts[0][...]
    for part in parts[1:]:
        total = total + part[...]
    if first:
        residual = total
    else:
        onsager = total[:, rows : rows + 1] / all_rows
        residual = measured[...] - total + onsager * old[...]
    residual_out[...] = residual
    columns = jnp.broadcast_to(residual, (LANES, residual.shape[1])).T

    def step(group, carry):
        start = pl.multiple_of(group * UNROLL * LANES, UNROLL * LANES)
        sums = [jnp.zeros((8, LANES), jnp.float32)] * UNROLL
        for at in range(0, rows, 8):
            block = sensing[pl.ds(at, 8), pl.ds(start, UNROLL * LANES)]
            for tile in range(UNROLL):
                sums[tile] += block[:, tile * LANES : (tile + 1) * LANES] * columns[at : at + 8]
        out[pl.ds(pl.multiple_of(group * UNROLL, UNROLL), UNROLL), :] = jnp.concatenate(
            [jnp.sum(total, axis=0, keepdims=True) for total in sums]
        )
        return carry

    lax.fori_loop(0, out.shape[0] // UNROLL, step, 0)


def forward_kernel(first, rows, step_at, *refs):
    if first:
        thresholds, partial, other, sensing, estimate_out, out = refs
        pseudo = partial[...] + other[...]
    else:
        thresholds, partial, other, old, sensing, estimate_out, out = refs
        pseudo = old[...] + (partial[...] + other[...])
    estimate, slopes = shrink_and_slope(pseudo, thresholds[step_at])
    estimate_out[...] = estimate
    slope = jnp.sum(slopes, keepdims=True)

    def step(group, totals):
        start = pl.multiple_of(group * UNROLL * LANES, UNROLL * LANES)
        values = estimate_out[pl.ds(pl.multiple_of(group * UNROLL, UNROLL), UNROLL), :]
        spread = [jnp.broadcast_to(values[tile : tile + 1], (8, LANES)) for tile in range(UNROLL)]
        totals = list(totals)
        for at in range(0, rows, 8):
            block = sensing[pl.ds(at, 8), pl.ds(start, UNROLL * LANES)]
            for tile in range(UNROLL):
                totals[at // 8] += block[:, tile * LANES : (tile + 1) * LANES] * spread[tile]
        return tuple(totals)

    nothing = tuple(jnp.zeros((8, LANES), jnp.float32) for _ in range(rows // 8))
    totals = lax.fori_loop(0, estimate_out.shape[0] // UNROLL, step, nothing)
    total = jnp.concatenate(totals)
    padded = out.shape[1]
    total = jnp.concatenate([total, jnp.zeros((padded - rows, LANES), jnp.float32)])
    product = jnp.sum(total.T, axis=0, keepdims=True)
    place = lax.broadcasted_iota(jnp.int32, product.shape, 1)
    out[...] = jnp.where(place == rows, slope, product)


def on_device(sensing, measured, thresholds):
    rows, width = sensing.shape
    local_rows = measured.shape[0]
    devices = lax.axis_size("row")
    groups = devices // COLS
    all_rows = local_rows * devices
    low_bits = groups.bit_length() - 1
    index = lax.axis_index("row")
    group_pos = index % groups
    column_pos = index // groups
    share = width // groups
    padded = (rows + LANES) // LANES * LANES
    tiles = width // LANES
    params = pltpu.CompilerParams(vmem_limit_bytes=LIMIT)
    in_vmem = pl.BlockSpec(memory_space=VMEM)
    in_smem = pl.BlockSpec(memory_space=pltpu.SMEM)
    matrix = pl.pallas_call(
        load_kernel,
        out_shape=VMEM(sensing.shape, sensing.dtype),
        in_specs=[pl.BlockSpec(memory_space=pl.ANY)],
        out_specs=in_vmem,
        scratch_shapes=[pltpu.SemaphoreType.DMA(())],
        compiler_params=params,
        cost_estimate=pl.CostEstimate(
            flops=0, bytes_accessed=2 * sensing.size * 4, transcendentals=0
        ),
        name="load",
    )(sensing)
    matrix = pltpu.with_memory_space_constraint(matrix, VMEM)
    row = jax.ShapeDtypeStruct((1, padded), jnp.float32)
    signal = jax.ShapeDtypeStruct((tiles, LANES), jnp.float32)

    def back(first, parts, *others):
        return pl.pallas_call(
            functools.partial(back_kernel, first, rows, all_rows),
            out_shape=(signal, row),
            in_specs=[in_vmem] * (len(parts) + len(others) + 1),
            out_specs=(in_vmem, in_vmem),
            compiler_params=params,
            name="back",
        )(*parts, *others, matrix)

    def forward(first, step, *others):
        return pl.pallas_call(
            functools.partial(forward_kernel, first, rows, step),
            out_shape=(signal, row),
            in_specs=[in_smem] + [in_vmem] * (len(others) + 1),
            out_specs=(in_vmem, in_vmem),
            compiler_params=params,
            name="forward",
        )(thresholds, *others, matrix)

    def all_columns(piece):
        flat = piece.reshape(padded)
        return [piece] + [
            swapped(flat, groups * mask).reshape(1, padded) for mask in range(1, COLS)
        ]

    own = lax.dynamic_update_slice(
        jnp.zeros((padded,), jnp.float32), measured, (column_pos * local_rows,)
    ).reshape(1, padded)
    parts = all_columns(own)
    others = ()
    estimate = ()
    for step in range(ITERS):
        partial, residual = back(step == 0, parts, *others)
        if step == 0:
            measured_row = residual
        others = (measured_row, residual)
        flat = partial.reshape(width)
        for position in range(low_bits - 1):
            flat = flat + swapped(flat, 2**position)
        other = swapped(flat, 2 ** (low_bits - 1))
        shaped = (tiles, LANES)
        new_estimate, product = forward(
            step == 0, step, flat.reshape(shaped), other.reshape(shaped), *estimate
        )
        estimate = (new_estimate,)
        parts = all_columns(product)
    total = sum(parts[1:], parts[0])[0]
    onsager = total[rows] / all_rows
    final = measured_row[0] - total + onsager * others[1][0]
    estimate = lax.dynamic_slice_in_dim(estimate[0].reshape(width), group_pos * share, share)
    residual = lax.dynamic_slice_in_dim(final, column_pos * local_rows, local_rows)
    return (estimate, residual)


def solution(mesh):
    in_specs = (P("row", None), P(("grp", "row")), P("grp"))
    out_specs = (P(("grp", "row")), P(("grp", "row")))
    return jax.shard_map(
        on_device, mesh=mesh, in_specs=in_specs, out_specs=out_specs, check_vma=False
    )
```

```python
import functools

import jax
import jax.numpy as jnp
from jax import lax
from jax.experimental import pallas as pl
from jax.experimental.pallas import tpu as pltpu
from jax.sharding import PartitionSpec as P

COLS = 4
ITERS = 6
SOFTNESS = 0.25
LANES = 128
UNROLL = 16
VMEM = pltpu.VMEM
LIMIT = 40 * 2**20
ATANH = (
    0.999999999783453,
    0.3333334145023831,
    0.1999927837517024,
    0.14311218617609153,
    0.10693692054721207,
    0.1220053340626646,
)


def swapped(value, mask):
    pairs = [(source, source ^ mask) for source in range(lax.axis_size("row"))]
    return lax.ppermute(value, "row", pairs)


def shrink_and_slope(values, level):
    scaled = jnp.abs(values) * (1.0 / SOFTNESS)
    scaled_level = level * (1.0 / SOFTNESS)
    gap = scaled - scaled_level
    upper = jnp.exp(-jnp.abs(gap))
    lower = jnp.exp(-(scaled + scaled_level))
    one, two = 1.0 + upper, 2.0 + upper
    inverse = 1.0 / (one * two)
    ratio = upper * (one * inverse)
    square = ratio * ratio
    series = ATANH[-1]
    for coefficient in ATANH[-2::-1]:
        series = series * square + coefficient
    upper_log = (ratio + ratio) * series
    lower_log = lower * (1.0 - lower * (0.5 - lower * (1.0 / 3.0)))
    size = SOFTNESS * (jnp.maximum(gap, 0.0) + (upper_log - lower_log))
    estimate = jnp.where(values < 0.0, -size, jnp.where(values > 0.0, size, 0.0))
    slope = jnp.where(gap >= 0.0, 1.0, upper) * (two * inverse) + lower * (1.0 - lower * (1.0 - lower))
    return estimate, slope


def column_total(parts):
    while len(parts) > 1:
        parts = [parts[at] + parts[at + 1] for at in range(0, len(parts), 2)]
    return parts[0]


def load_kernel(source, target, semaphore):
    copy = pltpu.make_async_copy(source, target, semaphore)
    copy.start()
    copy.wait()


def back_kernel(first, rows, all_rows, *refs):
    if first:
        *parts, sensing, out, residual_out = refs
    else:
        *parts, measured, old, sensing, out, residual_out = refs
    total = column_total([part[...] for part in parts])
    if first:
        residual = total
    else:
        onsager = total[:, rows : rows + 1] / all_rows
        residual = measured[...] - total + onsager * old[...]
    residual_out[...] = residual
    columns = jnp.broadcast_to(residual, (LANES, residual.shape[1])).T

    def step(group, carry):
        start = pl.multiple_of(group * UNROLL * LANES, UNROLL * LANES)
        sums = [jnp.zeros((8, LANES), jnp.float32)] * UNROLL
        for at in range(0, rows, 8):
            block = sensing[pl.ds(at, 8), pl.ds(start, UNROLL * LANES)]
            for tile in range(UNROLL):
                sums[tile] += block[:, tile * LANES : (tile + 1) * LANES] * columns[at : at + 8]
        out[pl.ds(pl.multiple_of(group * UNROLL, UNROLL), UNROLL), :] = jnp.concatenate(
            [jnp.sum(total, axis=0, keepdims=True) for total in sums]
        )
        return carry

    lax.fori_loop(0, out.shape[0] // UNROLL, step, 0)


def forward_kernel(first, rows, step_at, *refs):
    if first:
        thresholds, partial, other, sensing, estimate_out, out = refs
        pseudo = partial[...] + other[...]
    else:
        thresholds, partial, other, old, sensing, estimate_out, out = refs
        pseudo = old[...] + (partial[...] + other[...])
    estimate, slopes = shrink_and_slope(pseudo, thresholds[:, step_at : step_at + 1])
    estimate_out[...] = estimate
    slope = jnp.sum(slopes, axis=0, keepdims=True)

    def step(group, totals):
        start = pl.multiple_of(group * UNROLL * LANES, UNROLL * LANES)
        values = estimate_out[pl.ds(pl.multiple_of(group * UNROLL, UNROLL), UNROLL), :]
        spread = [jnp.broadcast_to(values[tile : tile + 1], (8, LANES)) for tile in range(UNROLL)]
        totals = list(totals)
        for at in range(0, rows, 8):
            block = sensing[pl.ds(at, 8), pl.ds(start, UNROLL * LANES)]
            for tile in range(UNROLL):
                totals[at // 8] += block[:, tile * LANES : (tile + 1) * LANES] * spread[tile]
        return tuple(totals)

    nothing = tuple(jnp.zeros((8, LANES), jnp.float32) for _ in range(rows // 8))
    totals = lax.fori_loop(0, estimate_out.shape[0] // UNROLL, step, nothing)
    padding = jnp.zeros((out.shape[1] - rows - 8, LANES), jnp.float32)
    total = jnp.concatenate([*totals, jnp.broadcast_to(slope, (8, LANES)), padding])
    out[...] = jnp.sum(total.T, axis=0, keepdims=True)


def on_device(sensing, measured, thresholds):
    rows, width = sensing.shape
    local_rows = measured.shape[0]
    devices = lax.axis_size("row")
    groups = devices // COLS
    all_rows = local_rows * devices
    low_bits = groups.bit_length() - 1
    index = lax.axis_index("row")
    group_pos = index % groups
    column_pos = index // groups
    share = width // groups
    padded = (rows + 8 + LANES - 1) // LANES * LANES
    tiles = width // LANES
    params = pltpu.CompilerParams(vmem_limit_bytes=LIMIT)
    in_vmem = pl.BlockSpec(memory_space=VMEM)
    matrix = pl.pallas_call(
        load_kernel,
        out_shape=VMEM(sensing.shape, sensing.dtype),
        in_specs=[pl.BlockSpec(memory_space=pl.ANY)],
        out_specs=in_vmem,
        scratch_shapes=[pltpu.SemaphoreType.DMA(())],
        compiler_params=params,
        cost_estimate=pl.CostEstimate(
            flops=0, bytes_accessed=2 * sensing.size * 4, transcendentals=0
        ),
        name="load",
    )(sensing)
    matrix = pltpu.with_memory_space_constraint(matrix, VMEM)
    row = jax.ShapeDtypeStruct((1, padded), jnp.float32)
    signal = jax.ShapeDtypeStruct((tiles, LANES), jnp.float32)

    def back(first, parts, *others):
        return pl.pallas_call(
            functools.partial(back_kernel, first, rows, all_rows),
            out_shape=(signal, row),
            in_specs=[in_vmem] * (len(parts) + len(others) + 1),
            out_specs=(in_vmem, in_vmem),
            compiler_params=params,
            name="back",
        )(*parts, *others, matrix)

    def forward(first, step, *others):
        return pl.pallas_call(
            functools.partial(forward_kernel, first, rows, step),
            out_shape=(signal, row),
            in_specs=[in_vmem] * (len(others) + 2),
            out_specs=(in_vmem, in_vmem),
            compiler_params=params,
            name="forward",
        )(thresholds.reshape(1, -1), *others, matrix)

    def all_columns(piece):
        flat = piece.reshape(padded)
        return [piece] + [
            swapped(flat, groups * mask).reshape(1, padded) for mask in range(1, COLS)
        ]

    own = lax.dynamic_update_slice(
        jnp.zeros((padded,), jnp.float32), measured, (column_pos * local_rows,)
    ).reshape(1, padded)
    parts = all_columns(own)
    others = ()
    estimate = ()
    for step in range(ITERS):
        partial, residual = back(step == 0, parts, *others)
        if step == 0:
            measured_row = residual
        others = (measured_row, residual)
        flat = partial.reshape(width)
        for position in range(low_bits - 1):
            flat = flat + swapped(flat, 2**position)
        other = swapped(flat, 2 ** (low_bits - 1))
        shaped = (tiles, LANES)
        new_estimate, product = forward(
            step == 0, step, flat.reshape(shaped), other.reshape(shaped), *estimate
        )
        estimate = (new_estimate,)
        parts = all_columns(product)
    total = column_total(parts)[0]
    onsager = total[rows] / all_rows
    final = measured_row[0] - total + onsager * others[1][0]
    estimate = lax.dynamic_slice_in_dim(estimate[0].reshape(width), group_pos * share, share)
    residual = lax.dynamic_slice_in_dim(final, column_pos * local_rows, local_rows)
    return (estimate, residual)


def solution(mesh):
    in_specs = (P("row", None), P(("grp", "row")), P("grp"))
    out_specs = (P(("grp", "row")), P(("grp", "row")))
    return jax.shard_map(
        on_device, mesh=mesh, in_specs=in_specs, out_specs=out_specs, check_vma=False
    )
```

```python
import functools

import jax
import jax.numpy as jnp
from jax import lax
from jax.experimental import pallas as pl
from jax.experimental.pallas import tpu as pltpu
from jax.sharding import PartitionSpec as P

COLS = 4
ITERS = 6
SOFTNESS = 0.25
LANES = 128
UNROLL = 16
VMEM = pltpu.VMEM
LIMIT = 40 * 2**20
ATANH = (
    0.999999999783453,
    0.3333334145023831,
    0.1999927837517024,
    0.14311218617609153,
    0.10693692054721207,
    0.1220053340626646,
)


def swapped(value, mask):
    pairs = [(source, source ^ mask) for source in range(lax.axis_size("row"))]
    return lax.ppermute(value, "row", pairs)


def shrink_and_slope(values, level):
    scaled = jnp.abs(values) * (1.0 / SOFTNESS)
    scaled_level = level * (1.0 / SOFTNESS)
    gap = scaled - scaled_level
    upper = jnp.exp(-jnp.abs(gap))
    lower = jnp.exp(-(scaled + scaled_level))
    one, two = 1.0 + upper, 2.0 + upper
    inverse = 1.0 / (one * two)
    ratio = upper * (one * inverse)
    square = ratio * ratio
    series = ATANH[-1]
    for coefficient in ATANH[-2::-1]:
        series = series * square + coefficient
    upper_log = (ratio + ratio) * series
    lower_log = lower * (1.0 - lower * (0.5 - lower * (1.0 / 3.0)))
    size = SOFTNESS * (jnp.maximum(gap, 0.0) + (upper_log - lower_log))
    estimate = jnp.where(values < 0.0, -size, jnp.where(values > 0.0, size, 0.0))
    slope = jnp.where(gap >= 0.0, 1.0, upper) * (two * inverse) + lower * (1.0 - lower * (1.0 - lower))
    return estimate, slope


def column_total(parts):
    while len(parts) > 1:
        parts = [parts[at] + parts[at + 1] for at in range(0, len(parts), 2)]
    return parts[0]


def load_kernel(source, target, semaphore):
    copy = pltpu.make_async_copy(source, target, semaphore)
    copy.start()
    copy.wait()


def column_position():
    return lax.axis_index("row") // (lax.axis_size("row") // COLS)


def placed(piece, position, padded):
    rest = jnp.zeros((1, padded - piece.shape[1]), jnp.float32)
    return pltpu.roll(jnp.concatenate([piece, rest], axis=1), position * piece.shape[1], 1)


def new_residual(pieces, measured, old, rows, all_rows):
    total = column_total([piece[...] for piece in pieces])
    onsager = total[:, rows : rows + 1] / all_rows
    return measured[...] - total + onsager * old[...]


def last_kernel(rows, all_rows, *refs):
    *pieces, measured, old, out = refs
    residual = new_residual(pieces, measured, old, rows, all_rows)
    padded, own = residual.shape[1], out.shape[1]
    out[...] = pltpu.roll(residual, padded - column_position() * own, 1)[:, :own]


def back_kernel(first, rows, all_rows, *refs):
    if first:
        *parts, sensing, out, residual_out = refs
    else:
        *parts, measured, old, sensing, out, residual_out = refs
    total = column_total([part[...] for part in parts])
    if first:
        residual = total
    else:
        onsager = total[:, rows : rows + 1] / all_rows
        residual = measured[...] - total + onsager * old[...]
    residual_out[...] = residual
    columns = jnp.broadcast_to(residual, (LANES, residual.shape[1])).T

    def step(group, carry):
        start = pl.multiple_of(group * UNROLL * LANES, UNROLL * LANES)
        sums = [jnp.zeros((8, LANES), jnp.float32)] * UNROLL
        for at in range(0, rows, 8):
            block = sensing[pl.ds(at, 8), pl.ds(start, UNROLL * LANES)]
            for tile in range(UNROLL):
                sums[tile] += block[:, tile * LANES : (tile + 1) * LANES] * columns[at : at + 8]
        out[pl.ds(pl.multiple_of(group * UNROLL, UNROLL), UNROLL), :] = jnp.concatenate(
            [jnp.sum(total, axis=0, keepdims=True) for total in sums]
        )
        return carry

    lax.fori_loop(0, out.shape[0] // UNROLL, step, 0)


def forward_kernel(first, rows, step_at, *refs):
    if first:
        thresholds, partial, other, sensing, estimate_out, out = refs
        pseudo = partial[...] + other[...]
    else:
        thresholds, partial, other, old, sensing, estimate_out, out = refs
        pseudo = old[...] + (partial[...] + other[...])
    estimate, slopes = shrink_and_slope(pseudo, thresholds[:, step_at : step_at + 1])
    estimate_out[...] = estimate
    slope = jnp.sum(slopes, axis=0, keepdims=True)

    def step(group, totals):
        start = pl.multiple_of(group * UNROLL * LANES, UNROLL * LANES)
        values = estimate_out[pl.ds(pl.multiple_of(group * UNROLL, UNROLL), UNROLL), :]
        spread = [jnp.broadcast_to(values[tile : tile + 1], (8, LANES)) for tile in range(UNROLL)]
        totals = list(totals)
        for at in range(0, rows, 8):
            block = sensing[pl.ds(at, 8), pl.ds(start, UNROLL * LANES)]
            for tile in range(UNROLL):
                totals[at // 8] += block[:, tile * LANES : (tile + 1) * LANES] * spread[tile]
        return tuple(totals)

    nothing = tuple(jnp.zeros((8, LANES), jnp.float32) for _ in range(rows // 8))
    totals = lax.fori_loop(0, estimate_out.shape[0] // UNROLL, step, nothing)
    padding = jnp.zeros((out.shape[1] - rows - 8, LANES), jnp.float32)
    total = jnp.concatenate([*totals, jnp.broadcast_to(slope, (8, LANES)), padding])
    out[...] = jnp.sum(total.T, axis=0, keepdims=True)


def on_device(sensing, measured, thresholds):
    rows, width = sensing.shape
    local_rows = measured.shape[0]
    devices = lax.axis_size("row")
    groups = devices // COLS
    all_rows = local_rows * devices
    low_bits = groups.bit_length() - 1
    index = lax.axis_index("row")
    group_pos = index % groups
    column_pos = index // groups
    share = width // groups
    padded = (rows + 8 + LANES - 1) // LANES * LANES
    tiles = width // LANES
    params = pltpu.CompilerParams(vmem_limit_bytes=LIMIT)
    in_vmem = pl.BlockSpec(memory_space=VMEM)
    matrix = pl.pallas_call(
        load_kernel,
        out_shape=VMEM(sensing.shape, sensing.dtype),
        in_specs=[pl.BlockSpec(memory_space=pl.ANY)],
        out_specs=in_vmem,
        scratch_shapes=[pltpu.SemaphoreType.DMA(())],
        compiler_params=params,
        cost_estimate=pl.CostEstimate(
            flops=0, bytes_accessed=2 * sensing.size * 4, transcendentals=0
        ),
        name="load",
    )(sensing)
    matrix = pltpu.with_memory_space_constraint(matrix, VMEM)
    row = jax.ShapeDtypeStruct((1, padded), jnp.float32)
    signal = jax.ShapeDtypeStruct((tiles, LANES), jnp.float32)

    def back(first, parts, *others):
        return pl.pallas_call(
            functools.partial(back_kernel, first, rows, all_rows),
            out_shape=(signal, row),
            in_specs=[in_vmem] * (len(parts) + len(others) + 1),
            out_specs=(in_vmem, in_vmem),
            compiler_params=params,
            name="back",
        )(*parts, *others, matrix)

    def forward(first, step, *others):
        return pl.pallas_call(
            functools.partial(forward_kernel, first, rows, step),
            out_shape=(signal, row),
            in_specs=[in_vmem] * (len(others) + 2),
            out_specs=(in_vmem, in_vmem),
            compiler_params=params,
            name="forward",
        )(thresholds.reshape(1, -1), *others, matrix)

    def all_columns(piece):
        flat = piece.reshape(padded)
        return [piece] + [
            swapped(flat, groups * mask).reshape(1, padded) for mask in range(1, COLS)
        ]

    own = lax.dynamic_update_slice(
        jnp.zeros((padded,), jnp.float32), measured, (column_pos * local_rows,)
    ).reshape(1, padded)
    parts = all_columns(own)
    others = ()
    estimate = ()
    for step in range(ITERS):
        partial, residual = back(step == 0, parts, *others)
        if step == 0:
            measured_row = residual
        others = (measured_row, residual)
        flat = partial.reshape(width)
        for position in range(low_bits - 1):
            flat = flat + swapped(flat, 2**position)
        other = swapped(flat, 2 ** (low_bits - 1))
        shaped = (tiles, LANES)
        new_estimate, product = forward(
            step == 0, step, flat.reshape(shaped), other.reshape(shaped), *estimate
        )
        estimate = (new_estimate,)
        parts = all_columns(product)
    residual = pl.pallas_call(
        functools.partial(last_kernel, rows, all_rows),
        out_shape=jax.ShapeDtypeStruct((1, local_rows), jnp.float32),
        in_specs=[in_vmem] * (len(parts) + len(others)),
        out_specs=in_vmem,
        compiler_params=params,
        name="last",
    )(*parts, *others)
    estimate = lax.dynamic_slice_in_dim(estimate[0].reshape(width), group_pos * share, share)
    return (estimate, residual.reshape(local_rows))


def solution(mesh):
    in_specs = (P("row", None), P(("grp", "row")), P("grp"))
    out_specs = (P(("grp", "row")), P(("grp", "row")))
    return jax.shard_map(
        on_device, mesh=mesh, in_specs=in_specs, out_specs=out_specs, check_vma=False
    )
```

```python
import functools

import jax
import jax.numpy as jnp
from jax import lax
from jax.experimental import pallas as pl
from jax.experimental.pallas import tpu as pltpu
from jax.sharding import PartitionSpec as P

COLS = 4
ITERS = 6
SOFTNESS = 0.25
LANES = 128
UNROLL = 16
COLUMN_ORDER = (1, 2, 3)
ROW_ORDER = (3, 1, 2)
VMEM = pltpu.VMEM
LIMIT = 40 * 2**20
ATANH = (
    0.999999999783453,
    0.3333334145023831,
    0.1999927837517024,
    0.14311218617609153,
    0.10693692054721207,
    0.1220053340626646,
)


def swapped(value, mask):
    pairs = [(source, source ^ mask) for source in range(lax.axis_size("row"))]
    return lax.ppermute(value, "row", pairs)


def shrink_and_slope(values, level):
    scaled = jnp.abs(values) * (1.0 / SOFTNESS)
    scaled_level = level * (1.0 / SOFTNESS)
    gap = scaled - scaled_level
    upper = jnp.exp(-jnp.abs(gap))
    lower = jnp.exp(-(scaled + scaled_level))
    one, two = 1.0 + upper, 2.0 + upper
    inverse = 1.0 / (one * two)
    ratio = upper * (one * inverse)
    square = ratio * ratio
    series = ATANH[-1]
    for coefficient in ATANH[-2::-1]:
        series = series * square + coefficient
    upper_log = (ratio + ratio) * series
    lower_log = lower * (1.0 - lower * (0.5 - lower * (1.0 / 3.0)))
    size = SOFTNESS * (jnp.maximum(gap, 0.0) + (upper_log - lower_log))
    estimate = jnp.where(values < 0.0, -size, jnp.where(values > 0.0, size, 0.0))
    slope = jnp.where(gap >= 0.0, 1.0, upper) * (two * inverse) + lower * (1.0 - lower * (1.0 - lower))
    return estimate, slope


def exchanged(piece, unit, order):
    flat = piece.reshape(-1)
    return [piece] + [swapped(flat, unit * mask).reshape(piece.shape) for mask in order]


def pairwise_total(pieces, order):
    by_mask = dict(zip((0, *order), pieces))
    parts = [by_mask[mask][...] for mask in range(len(by_mask))]
    while len(parts) > 1:
        parts = [parts[at] + parts[at + 1] for at in range(0, len(parts), 2)]
    return parts[0]


def load_kernel(source, target, semaphore):
    copy = pltpu.make_async_copy(source, target, semaphore)
    copy.start()
    copy.wait()


def column_position():
    return lax.axis_index("row") // (lax.axis_size("row") // COLS)


def placed(piece, position, padded):
    rest = jnp.zeros((1, padded - piece.shape[1]), jnp.float32)
    return pltpu.roll(jnp.concatenate([piece, rest], axis=1), position * piece.shape[1], 1)


def new_residual(pieces, measured, old, rows, all_rows):
    total = pairwise_total(pieces, COLUMN_ORDER)
    onsager = total[:, rows : rows + 1] / all_rows
    return measured[...] - total + onsager * old[...]


def last_kernel(rows, all_rows, *refs):
    *pieces, measured, old, out = refs
    residual = new_residual(pieces, measured, old, rows, all_rows)
    padded, own = residual.shape[1], out.shape[1]
    out[...] = pltpu.roll(residual, padded - column_position() * own, 1)[:, :own]


def back_kernel(first, rows, all_rows, *refs):
    if first:
        *parts, sensing, out, residual_out = refs
    else:
        *parts, measured, old, sensing, out, residual_out = refs
    total = pairwise_total(parts, COLUMN_ORDER)
    if first:
        residual = total
    else:
        onsager = total[:, rows : rows + 1] / all_rows
        residual = measured[...] - total + onsager * old[...]
    residual_out[...] = residual
    columns = jnp.broadcast_to(residual, (LANES, residual.shape[1])).T

    def step(group, carry):
        start = pl.multiple_of(group * UNROLL * LANES, UNROLL * LANES)
        sums = [jnp.zeros((8, LANES), jnp.float32)] * UNROLL
        for at in range(0, rows, 8):
            block = sensing[pl.ds(at, 8), pl.ds(start, UNROLL * LANES)]
            for tile in range(UNROLL):
                sums[tile] += block[:, tile * LANES : (tile + 1) * LANES] * columns[at : at + 8]
        out[pl.ds(pl.multiple_of(group * UNROLL, UNROLL), UNROLL), :] = jnp.concatenate(
            [jnp.sum(total, axis=0, keepdims=True) for total in sums]
        )
        return carry

    lax.fori_loop(0, out.shape[0] // UNROLL, step, 0)


def forward_kernel(first, rows, step_at, order, *refs):
    thresholds, *pieces, sensing, estimate_out, out = refs
    pseudo = pairwise_total(pieces[: len(order) + 1], order)
    if not first:
        pseudo = pieces[-1][...] + pseudo
    estimate, slopes = shrink_and_slope(pseudo, thresholds[:, step_at : step_at + 1])
    estimate_out[...] = estimate
    slope = jnp.sum(slopes, axis=0, keepdims=True)

    def step(group, totals):
        start = pl.multiple_of(group * UNROLL * LANES, UNROLL * LANES)
        values = estimate_out[pl.ds(pl.multiple_of(group * UNROLL, UNROLL), UNROLL), :]
        spread = [jnp.broadcast_to(values[tile : tile + 1], (8, LANES)) for tile in range(UNROLL)]
        totals = list(totals)
        for at in range(0, rows, 8):
            block = sensing[pl.ds(at, 8), pl.ds(start, UNROLL * LANES)]
            for tile in range(UNROLL):
                totals[at // 8] += block[:, tile * LANES : (tile + 1) * LANES] * spread[tile]
        return tuple(totals)

    nothing = tuple(jnp.zeros((8, LANES), jnp.float32) for _ in range(rows // 8))
    totals = lax.fori_loop(0, estimate_out.shape[0] // UNROLL, step, nothing)
    padding = jnp.zeros((out.shape[1] - rows - 8, LANES), jnp.float32)
    total = jnp.concatenate([*totals, jnp.broadcast_to(slope, (8, LANES)), padding])
    out[...] = jnp.sum(total.T, axis=0, keepdims=True)


def on_device(sensing, measured, thresholds):
    rows, width = sensing.shape
    local_rows = measured.shape[0]
    devices = lax.axis_size("row")
    groups = devices // COLS
    all_rows = local_rows * devices
    low_bits = groups.bit_length() - 1
    direct = min(low_bits, 2)
    row_order = tuple(mask for mask in ROW_ORDER if mask < 2**direct)
    index = lax.axis_index("row")
    group_pos = index % groups
    column_pos = index // groups
    share = width // groups
    padded = (rows + 8 + LANES - 1) // LANES * LANES
    tiles = width // LANES
    params = pltpu.CompilerParams(vmem_limit_bytes=LIMIT)
    in_vmem = pl.BlockSpec(memory_space=VMEM)
    matrix = pl.pallas_call(
        load_kernel,
        out_shape=VMEM(sensing.shape, sensing.dtype),
        in_specs=[pl.BlockSpec(memory_space=pl.ANY)],
        out_specs=in_vmem,
        scratch_shapes=[pltpu.SemaphoreType.DMA(())],
        compiler_params=params,
        cost_estimate=pl.CostEstimate(
            flops=0, bytes_accessed=2 * sensing.size * 4, transcendentals=0
        ),
        name="load",
    )(sensing)
    matrix = pltpu.with_memory_space_constraint(matrix, VMEM)
    row = jax.ShapeDtypeStruct((1, padded), jnp.float32)
    signal = jax.ShapeDtypeStruct((tiles, LANES), jnp.float32)

    def back(first, parts, *others):
        return pl.pallas_call(
            functools.partial(back_kernel, first, rows, all_rows),
            out_shape=(signal, row),
            in_specs=[in_vmem] * (len(parts) + len(others) + 1),
            out_specs=(in_vmem, in_vmem),
            compiler_params=params,
            name="back",
        )(*parts, *others, matrix)

    def forward(first, step, *others):
        return pl.pallas_call(
            functools.partial(forward_kernel, first, rows, step, row_order),
            out_shape=(signal, row),
            in_specs=[in_vmem] * (len(others) + 2),
            out_specs=(in_vmem, in_vmem),
            compiler_params=params,
            name="forward",
        )(thresholds.reshape(1, -1), *others, matrix)

    own = lax.dynamic_update_slice(
        jnp.zeros((padded,), jnp.float32), measured, (column_pos * local_rows,)
    ).reshape(1, padded)
    parts = exchanged(own, groups, COLUMN_ORDER)
    others = ()
    estimate = ()
    for step in range(ITERS):
        partial, residual = back(step == 0, parts, *others)
        if step == 0:
            measured_row = residual
        others = (measured_row, residual)
        for position in range(low_bits - direct):
            partial = sum(exchanged(partial, 2**position, (1,)))
        sent = exchanged(partial, groups >> direct, row_order)
        new_estimate, product = forward(step == 0, step, *sent, *estimate)
        estimate = (new_estimate,)
        parts = exchanged(product, groups, COLUMN_ORDER)
    residual = pl.pallas_call(
        functools.partial(last_kernel, rows, all_rows),
        out_shape=jax.ShapeDtypeStruct((1, local_rows), jnp.float32),
        in_specs=[in_vmem] * (len(parts) + len(others)),
        out_specs=in_vmem,
        compiler_params=params,
        name="last",
    )(*parts, *others)
    estimate = lax.dynamic_slice_in_dim(estimate[0].reshape(width), group_pos * share, share)
    return (estimate, residual.reshape(local_rows))


def solution(mesh):
    in_specs = (P("row", None), P(("grp", "row")), P("grp"))
    out_specs = (P(("grp", "row")), P(("grp", "row")))
    return jax.shard_map(
        on_device, mesh=mesh, in_specs=in_specs, out_specs=out_specs, check_vma=False
    )
```

```python
import functools

import jax
import jax.numpy as jnp
from jax import lax
from jax.experimental import pallas as pl
from jax.experimental.pallas import tpu as pltpu
from jax.sharding import PartitionSpec as P

COLS = 4
ITERS = 6
SOFTNESS = 0.25
LANES = 128
UNROLL = 16
COLUMN_ORDER = (1, 2, 3)
ROW_ORDER = (3, 1, 2)
GATHER_ORDER = (1, 3, 2)
VMEM = pltpu.VMEM
LIMIT = 40 * 2**20
ATANH = (
    0.999999999783453,
    0.3333334145023831,
    0.1999927837517024,
    0.14311218617609153,
    0.10693692054721207,
    0.1220053340626646,
)


def swapped(value, mask):
    pairs = [(source, source ^ mask) for source in range(lax.axis_size("row"))]
    return lax.ppermute(value, "row", pairs)


def shrink_and_slope(values, level):
    scaled = jnp.abs(values) * (1.0 / SOFTNESS)
    scaled_level = level * (1.0 / SOFTNESS)
    gap = scaled - scaled_level
    upper = jnp.exp(-jnp.abs(gap))
    lower = jnp.exp(-(scaled + scaled_level))
    one, two = 1.0 + upper, 2.0 + upper
    inverse = 1.0 / (one * two)
    ratio = upper * (one * inverse)
    square = ratio * ratio
    series = ATANH[-1]
    for coefficient in ATANH[-2::-1]:
        series = series * square + coefficient
    upper_log = (ratio + ratio) * series
    lower_log = lower * (1.0 - lower * (0.5 - lower * (1.0 / 3.0)))
    size = SOFTNESS * (jnp.maximum(gap, 0.0) + (upper_log - lower_log))
    estimate = jnp.where(values < 0.0, -size, jnp.where(values > 0.0, size, 0.0))
    slope = jnp.where(gap >= 0.0, 1.0, upper) * (two * inverse) + lower * (1.0 - lower * (1.0 - lower))
    return estimate, slope


def exchanged(piece, unit, order):
    flat = piece.reshape(-1)
    return [piece] + [swapped(flat, unit * mask).reshape(piece.shape) for mask in order]


def pairwise_total(pieces, order):
    by_mask = dict(zip((0, *order), pieces))
    parts = [by_mask[mask][...] for mask in range(len(by_mask))]
    while len(parts) > 1:
        parts = [parts[at] + parts[at + 1] for at in range(0, len(parts), 2)]
    return parts[0]


def load_kernel(source, target, semaphore):
    copy = pltpu.make_async_copy(source, target, semaphore)
    copy.start()
    copy.wait()


def column_position():
    return lax.axis_index("row") // (lax.axis_size("row") // COLS)


def placed(piece, position, padded):
    rest = jnp.zeros((1, padded - piece.shape[1]), jnp.float32)
    return pltpu.roll(jnp.concatenate([piece, rest], axis=1), position * piece.shape[1], 1)


def new_residual(pieces, measured, old, rows, all_rows):
    total = pairwise_total(pieces, COLUMN_ORDER)
    onsager = total[:, rows : rows + 1] / all_rows
    return measured[...] - total + onsager * old[...]


def last_kernel(rows, all_rows, *refs):
    *pieces, measured, old, out = refs
    residual = new_residual(pieces, measured, old, rows, all_rows)
    padded, own = residual.shape[1], out.shape[1]
    out[...] = pltpu.roll(residual, padded - column_position() * own, 1)[:, :own]


def back_kernel(first, rows, all_rows, *refs):
    if first:
        *parts, sensing, out, residual_out = refs
    else:
        *parts, measured, old, sensing, out, residual_out = refs
    total = pairwise_total(parts, GATHER_ORDER if first else COLUMN_ORDER)
    if first:
        residual = total
    else:
        onsager = total[:, rows : rows + 1] / all_rows
        residual = measured[...] - total + onsager * old[...]
    residual_out[...] = residual
    columns = jnp.broadcast_to(residual, (LANES, residual.shape[1])).T

    def step(group, carry):
        start = pl.multiple_of(group * UNROLL * LANES, UNROLL * LANES)
        sums = [None] * UNROLL
        for at in range(0, rows, 8):
            block = sensing[pl.ds(at, 8), pl.ds(start, UNROLL * LANES)]
            for tile in range(UNROLL):
                term = block[:, tile * LANES : (tile + 1) * LANES] * columns[at : at + 8]
                sums[tile] = term if at == 0 else sums[tile] + term
        out[pl.ds(pl.multiple_of(group * UNROLL, UNROLL), UNROLL), :] = jnp.concatenate(
            [jnp.sum(total, axis=0, keepdims=True) for total in sums]
        )
        return carry

    lax.fori_loop(0, out.shape[0] // UNROLL, step, 0)


def forward_kernel(first, rows, step_at, order, *refs):
    thresholds, *pieces, sensing, estimate_out, out = refs
    pseudo = pairwise_total(pieces[: len(order) + 1], order)
    if not first:
        pseudo = pieces[-1][...] + pseudo
    estimate, slopes = shrink_and_slope(pseudo, thresholds[:, step_at : step_at + 1])
    estimate_out[...] = estimate
    slope = jnp.sum(slopes, axis=0, keepdims=True)

    def step(group, totals):
        start = pl.multiple_of(group * UNROLL * LANES, UNROLL * LANES)
        values = estimate_out[pl.ds(pl.multiple_of(group * UNROLL, UNROLL), UNROLL), :]
        spread = [jnp.broadcast_to(values[tile : tile + 1], (8, LANES)) for tile in range(UNROLL)]
        totals = list(totals)
        for at in range(0, rows, 8):
            block = sensing[pl.ds(at, 8), pl.ds(start, UNROLL * LANES)]
            for tile in range(UNROLL):
                totals[at // 8] += block[:, tile * LANES : (tile + 1) * LANES] * spread[tile]
        return tuple(totals)

    nothing = tuple(jnp.zeros((8, LANES), jnp.float32) for _ in range(rows // 8))
    totals = lax.fori_loop(0, estimate_out.shape[0] // UNROLL, step, nothing)
    padding = jnp.zeros((out.shape[1] - rows - 8, LANES), jnp.float32)
    total = jnp.concatenate([*totals, jnp.broadcast_to(slope, (8, LANES)), padding])
    out[...] = jnp.sum(total.T, axis=0, keepdims=True)


def on_device(sensing, measured, thresholds):
    rows, width = sensing.shape
    local_rows = measured.shape[0]
    devices = lax.axis_size("row")
    groups = devices // COLS
    all_rows = local_rows * devices
    low_bits = groups.bit_length() - 1
    direct = min(low_bits, 2)
    row_order = tuple(mask for mask in ROW_ORDER if mask < 2**direct)
    index = lax.axis_index("row")
    group_pos = index % groups
    column_pos = index // groups
    share = width // groups
    padded = (rows + 8 + LANES - 1) // LANES * LANES
    tiles = width // LANES
    params = pltpu.CompilerParams(vmem_limit_bytes=LIMIT)
    in_vmem = pl.BlockSpec(memory_space=VMEM)
    matrix = pl.pallas_call(
        load_kernel,
        out_shape=VMEM(sensing.shape, sensing.dtype),
        in_specs=[pl.BlockSpec(memory_space=pl.ANY)],
        out_specs=in_vmem,
        scratch_shapes=[pltpu.SemaphoreType.DMA(())],
        compiler_params=params,
        cost_estimate=pl.CostEstimate(
            flops=0, bytes_accessed=2 * sensing.size * 4, transcendentals=0
        ),
        name="load",
    )(sensing)
    matrix = pltpu.with_memory_space_constraint(matrix, VMEM)
    row = jax.ShapeDtypeStruct((1, padded), jnp.float32)
    signal = jax.ShapeDtypeStruct((tiles, LANES), jnp.float32)

    def back(first, parts, *others):
        return pl.pallas_call(
            functools.partial(back_kernel, first, rows, all_rows),
            out_shape=(signal, row),
            in_specs=[in_vmem] * (len(parts) + len(others) + 1),
            out_specs=(in_vmem, in_vmem),
            compiler_params=params,
            name="back",
        )(*parts, *others, matrix)

    def forward(first, step, *others):
        return pl.pallas_call(
            functools.partial(forward_kernel, first, rows, step, row_order),
            out_shape=(signal, row),
            in_specs=[in_vmem] * (len(others) + 2),
            out_specs=(in_vmem, in_vmem),
            compiler_params=params,
            name="forward",
        )(thresholds.reshape(1, -1), *others, matrix)

    own = jnp.concatenate(
        [jnp.where(index // groups == at, measured, 0.0) for at in range(COLS)]
        + [jnp.zeros((padded - COLS * local_rows,), jnp.float32)]
    ).reshape(1, padded)
    parts = exchanged(own, groups, GATHER_ORDER)
    others = ()
    estimate = ()
    for step in range(ITERS):
        partial, residual = back(step == 0, parts, *others)
        if step == 0:
            measured_row = residual
        others = (measured_row, residual)
        for position in range(low_bits - direct):
            partial = sum(exchanged(partial, 2**position, (1,)))
        sent = exchanged(partial, groups >> direct, row_order)
        new_estimate, product = forward(step == 0, step, *sent, *estimate)
        estimate = (new_estimate,)
        parts = exchanged(product, groups, COLUMN_ORDER)
    residual = pl.pallas_call(
        functools.partial(last_kernel, rows, all_rows),
        out_shape=jax.ShapeDtypeStruct((1, local_rows), jnp.float32),
        in_specs=[in_vmem] * (len(parts) + len(others)),
        out_specs=in_vmem,
        compiler_params=params,
        name="last",
    )(*parts, *others)
    estimate = lax.dynamic_slice_in_dim(estimate[0].reshape(width), group_pos * share, share)
    return (estimate, residual.reshape(local_rows))


def solution(mesh):
    in_specs = (P("row", None), P(("grp", "row")), P("grp"))
    out_specs = (P(("grp", "row")), P(("grp", "row")))
    return jax.shard_map(
        on_device, mesh=mesh, in_specs=in_specs, out_specs=out_specs, check_vma=False
    )
```

```python
import functools

import jax
import jax.numpy as jnp
from jax import lax
from jax.experimental import pallas as pl
from jax.experimental.pallas import tpu as pltpu
from jax.sharding import PartitionSpec as P

COLS = 4
ITERS = 6
SOFTNESS = 0.25
LANES = 128
UNROLL = 16
BACK_UNROLL = 32
COLUMN_ORDER = (1, 2, 3)
ROW_ORDER = (3, 1, 2)
GATHER_ORDER = (1, 3, 2)
VMEM = pltpu.VMEM
LIMIT = 40 * 2**20
ATANH = (
    0.999999999783453,
    0.3333334145023831,
    0.1999927837517024,
    0.14311218617609153,
    0.10693692054721207,
    0.1220053340626646,
)


def swapped(value, mask):
    pairs = [(source, source ^ mask) for source in range(lax.axis_size("row"))]
    return lax.ppermute(value, "row", pairs)


def shrink_and_slope(values, level):
    scaled = jnp.abs(values) * (1.0 / SOFTNESS)
    scaled_level = level * (1.0 / SOFTNESS)
    gap = scaled - scaled_level
    upper = jnp.exp(-jnp.abs(gap))
    lower = jnp.exp(-(scaled + scaled_level))
    one, two = 1.0 + upper, 2.0 + upper
    inverse = 1.0 / (one * two)
    ratio = upper * (one * inverse)
    square = ratio * ratio
    series = ATANH[-1]
    for coefficient in ATANH[-2::-1]:
        series = series * square + coefficient
    upper_log = (ratio + ratio) * series
    lower_log = lower * (1.0 - lower * (0.5 - lower * (1.0 / 3.0)))
    size = SOFTNESS * (jnp.maximum(gap, 0.0) + (upper_log - lower_log))
    estimate = jnp.where(values < 0.0, -size, jnp.where(values > 0.0, size, 0.0))
    slope = jnp.where(gap >= 0.0, 1.0, upper) * (two * inverse) + lower * (1.0 - lower * (1.0 - lower))
    return estimate, slope


def exchanged(piece, unit, order):
    flat = piece.reshape(-1)
    return [piece] + [swapped(flat, unit * mask).reshape(piece.shape) for mask in order]


def pairwise_total(pieces, order):
    by_mask = dict(zip((0, *order), pieces))
    parts = [by_mask[mask][...] for mask in range(len(by_mask))]
    while len(parts) > 1:
        parts = [parts[at] + parts[at + 1] for at in range(0, len(parts), 2)]
    return parts[0]


def load_kernel(source, target, semaphore):
    copy = pltpu.make_async_copy(source, target, semaphore)
    copy.start()
    copy.wait()


def column_position():
    return lax.axis_index("row") // (lax.axis_size("row") // COLS)


def placed(piece, position, padded):
    rest = jnp.zeros((1, padded - piece.shape[1]), jnp.float32)
    return pltpu.roll(jnp.concatenate([piece, rest], axis=1), position * piece.shape[1], 1)


def new_residual(pieces, measured, old, rows, all_rows):
    total = pairwise_total(pieces, COLUMN_ORDER)
    onsager = total[:, rows : rows + 1] / all_rows
    return measured[...] - total + onsager * old[...]


def last_kernel(rows, all_rows, *refs):
    *pieces, measured, old, out = refs
    residual = new_residual(pieces, measured, old, rows, all_rows)
    padded, own = residual.shape[1], out.shape[1]
    out[...] = pltpu.roll(residual, padded - column_position() * own, 1)[:, :own]


def back_kernel(first, rows, all_rows, *refs):
    if first:
        *parts, sensing, out, residual_out = refs
    else:
        *parts, measured, old, sensing, out, residual_out = refs
    total = pairwise_total(parts, GATHER_ORDER if first else COLUMN_ORDER)
    if first:
        residual = total
    else:
        onsager = total[:, rows : rows + 1] / all_rows
        residual = measured[...] - total + onsager * old[...]
    residual_out[...] = residual
    columns = jnp.broadcast_to(residual, (LANES, residual.shape[1])).T

    def step(group, carry):
        start = pl.multiple_of(group * BACK_UNROLL * LANES, BACK_UNROLL * LANES)
        sums = [None] * BACK_UNROLL
        for at in range(0, rows, 8):
            block = sensing[pl.ds(at, 8), pl.ds(start, BACK_UNROLL * LANES)]
            for tile in range(BACK_UNROLL):
                term = block[:, tile * LANES : (tile + 1) * LANES] * columns[at : at + 8]
                sums[tile] = term if at == 0 else sums[tile] + term
        out[pl.ds(pl.multiple_of(group * BACK_UNROLL, BACK_UNROLL), BACK_UNROLL), :] = jnp.concatenate(
            [jnp.sum(total, axis=0, keepdims=True) for total in sums]
        )
        return carry

    lax.fori_loop(0, out.shape[0] // BACK_UNROLL, step, 0)


def forward_kernel(first, rows, step_at, order, *refs):
    thresholds, *pieces, sensing, estimate_out, out = refs
    pseudo = pairwise_total(pieces[: len(order) + 1], order)
    if not first:
        pseudo = pieces[-1][...] + pseudo
    estimate, slopes = shrink_and_slope(pseudo, thresholds[:, step_at : step_at + 1])
    estimate_out[...] = estimate
    slope = jnp.sum(slopes, axis=0, keepdims=True)

    def step(group, totals):
        start = pl.multiple_of(group * UNROLL * LANES, UNROLL * LANES)
        values = estimate_out[pl.ds(pl.multiple_of(group * UNROLL, UNROLL), UNROLL), :]
        spread = [jnp.broadcast_to(values[tile : tile + 1], (8, LANES)) for tile in range(UNROLL)]
        totals = list(totals)
        for at in range(0, rows, 8):
            block = sensing[pl.ds(at, 8), pl.ds(start, UNROLL * LANES)]
            for tile in range(UNROLL):
                totals[at // 8] += block[:, tile * LANES : (tile + 1) * LANES] * spread[tile]
        return tuple(totals)

    nothing = tuple(jnp.zeros((8, LANES), jnp.float32) for _ in range(rows // 8))
    totals = lax.fori_loop(0, estimate_out.shape[0] // UNROLL, step, nothing)
    padding = jnp.zeros((out.shape[1] - rows - 8, LANES), jnp.float32)
    total = jnp.concatenate([*totals, jnp.broadcast_to(slope, (8, LANES)), padding])
    out[...] = jnp.sum(total.T, axis=0, keepdims=True)


def on_device(sensing, measured, thresholds):
    rows, width = sensing.shape
    local_rows = measured.shape[0]
    devices = lax.axis_size("row")
    groups = devices // COLS
    all_rows = local_rows * devices
    low_bits = groups.bit_length() - 1
    direct = min(low_bits, 2)
    row_order = tuple(mask for mask in ROW_ORDER if mask < 2**direct)
    index = lax.axis_index("row")
    group_pos = index % groups
    column_pos = index // groups
    share = width // groups
    padded = (rows + 8 + LANES - 1) // LANES * LANES
    tiles = width // LANES
    params = pltpu.CompilerParams(vmem_limit_bytes=LIMIT)
    in_vmem = pl.BlockSpec(memory_space=VMEM)
    matrix = pl.pallas_call(
        load_kernel,
        out_shape=VMEM(sensing.shape, sensing.dtype),
        in_specs=[pl.BlockSpec(memory_space=pl.ANY)],
        out_specs=in_vmem,
        scratch_shapes=[pltpu.SemaphoreType.DMA(())],
        compiler_params=params,
        cost_estimate=pl.CostEstimate(
            flops=0, bytes_accessed=2 * sensing.size * 4, transcendentals=0
        ),
        name="load",
    )(sensing)
    matrix = pltpu.with_memory_space_constraint(matrix, VMEM)
    row = jax.ShapeDtypeStruct((1, padded), jnp.float32)
    signal = jax.ShapeDtypeStruct((tiles, LANES), jnp.float32)

    def back(first, parts, *others):
        return pl.pallas_call(
            functools.partial(back_kernel, first, rows, all_rows),
            out_shape=(signal, row),
            in_specs=[in_vmem] * (len(parts) + len(others) + 1),
            out_specs=(in_vmem, in_vmem),
            compiler_params=params,
            name="back",
        )(*parts, *others, matrix)

    def forward(first, step, *others):
        return pl.pallas_call(
            functools.partial(forward_kernel, first, rows, step, row_order),
            out_shape=(signal, row),
            in_specs=[in_vmem] * (len(others) + 2),
            out_specs=(in_vmem, in_vmem),
            compiler_params=params,
            name="forward",
        )(thresholds.reshape(1, -1), *others, matrix)

    own = jnp.concatenate(
        [jnp.where(index // groups == at, measured, 0.0) for at in range(COLS)]
        + [jnp.zeros((padded - COLS * local_rows,), jnp.float32)]
    ).reshape(1, padded)
    parts = exchanged(own, groups, GATHER_ORDER)
    others = ()
    estimate = ()
    for step in range(ITERS):
        partial, residual = back(step == 0, parts, *others)
        if step == 0:
            measured_row = residual
        others = (measured_row, residual)
        for position in range(low_bits - direct):
            partial = sum(exchanged(partial, 2**position, (1,)))
        sent = exchanged(partial, groups >> direct, row_order)
        new_estimate, product = forward(step == 0, step, *sent, *estimate)
        estimate = (new_estimate,)
        parts = exchanged(product, groups, COLUMN_ORDER)
    residual = pl.pallas_call(
        functools.partial(last_kernel, rows, all_rows),
        out_shape=jax.ShapeDtypeStruct((1, local_rows), jnp.float32),
        in_specs=[in_vmem] * (len(parts) + len(others)),
        out_specs=in_vmem,
        compiler_params=params,
        name="last",
    )(*parts, *others)
    estimate = lax.dynamic_slice_in_dim(estimate[0].reshape(width), group_pos * share, share)
    return (estimate, residual.reshape(local_rows))


def solution(mesh):
    in_specs = (P("row", None), P(("grp", "row")), P("grp"))
    out_specs = (P(("grp", "row")), P(("grp", "row")))
    return jax.shard_map(
        on_device, mesh=mesh, in_specs=in_specs, out_specs=out_specs, check_vma=False
    )
```
